32 devices in a mesh: groups: 2 (over x), ep: 16 (over z, y, core).
Axes of the slice: x: 2, y: 2, z: 4, core: 2. Of those that a mesh axis runs over, the one named last changes fastest.
Arguments:
- residual: bfloat16 [128, 7168], P(('groups', 'ep')), parts along dimension 0, may hold values from -6 to 6
- queries: bfloat16 [128, 128, 192], P('groups', 'ep'), parts along dimension 0, may hold values from -60 to 60
- new_kv: bfloat16 [128, 576], P(('groups', 'ep')), parts along dimension 0, may hold values from -6 to 6
- kv_cache: bfloat16 [64, 384, 576], P(('groups', 'ep')), parts along dimension 0, may hold values from -9 to 9
- lengths: int32 [64], P(('groups', 'ep')), parts along dimension 0, may hold values from 2 to 384, as said below
- w_uk: bfloat16 [128, 128, 512], P('ep'), may hold values from -0.5 to 0.5
- w_uv: bfloat16 [128, 512, 128], P('ep'), may hold values from -0.75 to 0.75
- w_out: bfloat16 [16384, 7168], P('ep'), may hold values from -0.09375 to 0.09375
- norm_gain: float32 [7168], replicated, may hold values from 0.5 to 1.5
- w_gate: bfloat16 [7168, 8192], P(None, 'ep'), may hold values from -0.0625 to 0.0625
- w_up: bfloat16 [7168, 8192], P(None, 'ep'), may hold values from -0.0625 to 0.0625
- w_down: bfloat16 [8192, 7168], P('ep'), may hold values from -0.375 to 0.375
- route_ids: int32 [128, 2], P(('groups', 'ep')), parts along dimension 0, may hold values from 0 to 7, all different within a row; in each aligned block of 4 rows (0 to 3, 4 to 7, ...) at most 2 rows name the same one
- route_gates: float32 [128, 2], P(('groups', 'ep')), parts along dimension 0, may hold values from 0.2 to 1
Outputs:
- attn_out: bfloat16 [128, 7168], P(('groups', 'ep')), parts along dimension 0
- moe_out: bfloat16 [128, 7168], P(('groups', 'ep')), parts along dimension 0
The draws below stay inside these ranges and needn't reach their ends.
There are 2 independent parts, one for each index of `groups`. The reference program is written for one: setup_inputs(seed, part) draws one part's arguments, and reference() takes and returns one part's arrays. A program takes and returns all parts, laid end to end along the dimension named above; an argument that names none is the same for every part. Nothing has to cross between parts.
Inputs may be any that keep to these rules, and one draw needn't show every extreme that they name: `lengths`: at least 2 valid slots; on every device some request uses all 384 slots. `route_ids`: each row names 2 different experts; among the rows of one device no expert is named more than 2 times.
All inputs are finite; a program needn't handle non-finite values.
Results may differ from the reference program's by a relative error of at most 0.013.
Values may be sent and summed in bfloat16 or wider, within the bound.
A program may use at most 128 MiB of HBM per device.

```python
import math
import jax
import jax.numpy as jnp
import numpy as np
from jax import lax

D = 7168
HEADS = 128
LAT = 512
NOPE = 128
ROPE = 64
VDIM = 128
EXP_HID = 1024
EXPERTS = 8
TOPK = 2
REQ_DEV = 2
LEN = 384
TOK_DEV = 4
CAP = 2
SPLIT = 2
HID_DEV = 512
TOKENS = 64
REQUESTS = 32
N_EP = 16


def draw_queries(key, part):
    key = jax.random.fold_in(key, 11)
    base = jax.random.truncated_normal(key, -6.0, 6.0, (TOKENS, HEADS, NOPE + ROPE), jnp.float32)
    return base.astype(jnp.bfloat16)


def draw_kv_cache(key, part):
    key = jax.random.fold_in(key, 13)
    base = jax.random.truncated_normal(key, -6.0, 6.0, (REQUESTS, LEN, LAT + ROPE), jnp.float32)
    return base.astype(jnp.bfloat16)


def draw_lengths(key, part):
    key = jax.random.fold_in(key, 5)
    drawn = jax.random.randint(key, (REQ_DEV * (REQUESTS // REQ_DEV),), 2, LEN + 1).astype(jnp.int32)
    drawn = drawn.reshape(REQUESTS // REQ_DEV, REQ_DEV)
    drawn = drawn.at[:, 0].set(LEN)
    drawn = drawn.at[0, 1].set(2)
    return drawn.reshape(REQUESTS).astype(jnp.int32)


def shard_levels(rng, extent, split, least, top_value):
    level, own = 1.0, jax.random.fold_in(rng, 6)
    for dim, shards_of in split:
        draws = jnp.exp(jax.random.uniform(jax.random.fold_in(own, dim), (shards_of,), jnp.float32, least / len(split), top_value / len(split)))
        level = level * jnp.repeat(draws, extent[dim] // shards_of).reshape([-1 if axis == dim else 1 for axis in range(len(extent))])
    return level


def routed_block(own_key, own, number, rows, count, top, bound, skew):
    order = jax.random.permutation(own_key, count)
    packed, common = shares(count, rows * top, bound, skew, True), shares(count, rows * top, bound, skew, False)
    places = jnp.arange(count)

    def named(sizes, offset_by):
        used = int((sizes > 0).sum())
        fixed = max(1, used // 4)
        passed = fixed + (places - fixed + offset_by * (used - fixed)) % max(1, count - fixed)
        return jnp.zeros((count,), jnp.int32).at[order[jnp.where(places < fixed, places, passed)]].set(jnp.asarray(sizes, jnp.int32))

    sizes = jnp.where(number % 4 == 0, named(packed, number // 4), named(common, number - number // 4 - 1))
    mixed = jax.random.permutation(jax.random.fold_in(own, 3), count)
    donor, sink = mixed[0:count // 2 * 2:2], mixed[1:count // 2 * 2:2]
    slack = jnp.minimum(sizes[donor] - 1, bound - sizes[sink]) // 2
    slack = jnp.where((donor == order[0]) | (sink == order[0]) | (sizes[sink] == 0), 0, jnp.maximum(slack, 0))
    passed = jax.random.randint(jax.random.fold_in(own, 4), (count // 2,), 0, 1 << 20) % (slack + 1)
    sizes = sizes.at[donor].add(-passed).at[sink].add(passed)
    labels = jnp.searchsorted(jnp.cumsum(sizes), jnp.arange(rows * top), side="right").astype(jnp.int32)
    table = labels.reshape(top, rows).T
    table = table[jax.random.permutation(jax.random.fold_in(own, 1), rows)]
    offset_by = jax.random.randint(jax.random.fold_in(own, 2), (rows, 1), 0, top)
    return jnp.take_along_axis(table, (jnp.arange(top)[None, :] + offset_by) % top, axis=1)


def shares(count, total, most, lean, full):
    loads = [(1 << 20) // math.isqrt(grade ** lean) + 1 for grade in range(1, count + 1)]
    largest = most if full else min(most, max(-(-total // count), total * loads[0] // sum(loads)))
    least = 1 if total - largest >= count - 1 else 0
    holding, surplus = [largest] + [least] * (count - 1), total - largest - least * (count - 1)
    while surplus > 0:
        movable = [i for i in range(1, count) if holding[i] < largest] or [i for i in range(1, count) if holding[i] < most]
        pool, left = sum([loads[i] for i in movable]), surplus
        for i in movable:
            extra = min(most - holding[i], max(1, left * loads[i] // pool), surplus)
            holding[i] = holding[i] + extra
            surplus = surplus - extra
    return np.array(holding)


def noise(own_key, shape, deviation, bound, shards=(), kind=jnp.bfloat16):
    entries = jax.random.normal(own_key, shape, jnp.float32) * deviation
    if len(shards) > 0:
        entries = shard_levels(own_key, shape, shards, -0.22, 0.18) * entries
    return jnp.clip(entries, min=-bound, max=bound).astype(kind)


def setup_inputs(seed: int = 0, part: int = 0) -> dict:
    splits = jax.random.split(jax.random.key(seed), 15)
    own_keys = jax.random.split(jax.random.fold_in(splits[14], part), 15)
    residual = noise(own_keys[0], (TOKENS, D), 1.0, 6.0, ((0, 16),))
    queries = draw_queries(jax.random.fold_in(jax.random.fold_in(splits[14], part), 71), part)
    new_kv = noise(own_keys[2], (TOKENS, LAT + ROPE), 1.0, 6.0, ((0, 16),))
    kv_cache = draw_kv_cache(jax.random.fold_in(jax.random.fold_in(splits[14], part), 71), part)
    lengths = draw_lengths(jax.random.fold_in(jax.random.fold_in(splits[14], part), 71), part)
    w_uk = noise(splits[5], (HEADS, NOPE, LAT), NOPE ** -0.5, 0.5, ((0, 16),))
    w_uv = noise(splits[6], (HEADS, LAT, VDIM), 64 ** -0.5, 0.75, ((0, 16),))
    w_out = noise(splits[7], (HEADS * VDIM, D), (HEADS * VDIM // 4) ** -0.5, 0.09375, ((0, 16),))
    norm_gain = jnp.clip(1.0 + 0.1 * jax.random.normal(splits[8], (D,), jnp.float32), 0.5, 1.5)
    w_gate = noise(splits[9], (D, EXPERTS * EXP_HID), D ** -0.5, 0.0625, ((1, 16),))
    w_up = noise(splits[10], (D, EXPERTS * EXP_HID), D ** -0.5, 0.0625, ((1, 16),))
    w_down = noise(splits[11], (EXPERTS * EXP_HID, D), (EXP_HID // 4) ** -0.5, 0.375, ((0, 16),))
    route_ids_keys = jax.random.split(jax.random.fold_in(own_keys[12], 1), TOKENS // TOK_DEV)
    route_ids_turns = jax.random.permutation(jax.random.fold_in(own_keys[12], 3), TOKENS // TOK_DEV)
    route_ids = jax.vmap(lambda own, number: routed_block(jax.random.fold_in(own_keys[12], 2), own, number, TOK_DEV, EXPERTS, TOPK, CAP, 2))(route_ids_keys, route_ids_turns).reshape((TOKENS, TOPK))
    route_gates = jnp.clip(0.2 + 0.8 * jax.random.uniform(own_keys[13], (TOKENS, TOPK), jnp.float32) ** shard_levels(own_keys[13], (TOKENS, TOPK), ((0, 16),), -0.2, 0.2), 0.2, 1.0)
    return {"residual": residual, "queries": queries, "new_kv": new_kv, "kv_cache": kv_cache, "lengths": lengths, "w_uk": w_uk, "w_uv": w_uv, "w_out": w_out, "norm_gain": norm_gain, "w_gate": w_gate, "w_up": w_up, "w_down": w_down, "route_ids": route_ids, "route_gates": route_gates}


def reference(residual, queries, new_kv, kv_cache, lengths, w_uk, w_uv, w_out, norm_gain, w_gate, w_up, w_down, route_ids, route_gates):
    width = LAT + ROPE
    q_lat = jnp.einsum('thn,hnc->thc', queries[:, :, :NOPE].astype(jnp.float32), w_uk.astype(jnp.float32)).astype(jnp.bfloat16)
    q_abs = jnp.concatenate([q_lat, queries[:, :, NOPE:]], axis=-1)
    q_req = q_abs.reshape(REQUESTS, 2 * HEADS, width)
    keys = jnp.concatenate([kv_cache, new_kv.reshape(REQUESTS, 2, width)], axis=1)
    scale = (NOPE + ROPE) ** (-0.5)
    scores = jnp.einsum('rqc,rkc->rqk', q_req.astype(jnp.float32), keys.astype(jnp.float32)) * scale
    position = jnp.arange(LEN + 2)
    draft = jnp.arange(2 * HEADS) // HEADS
    valid = jnp.where(position[None, None, :] < LEN, position[None, None, :] < lengths[:, None, None], (position - LEN)[None, None, :] <= draft[None, :, None])
    scores = jnp.where(valid, scores, -1e+30)
    highest = lax.optimization_barrier(jnp.max(scores, axis=-1, keepdims=True))
    powers = jnp.where(valid, jnp.exp(scores - highest), 0.0)
    probs = (powers / lax.optimization_barrier(jnp.sum(powers, axis=-1, keepdims=True))).astype(jnp.bfloat16)
    latent = jnp.einsum('rqk,rkc->rqc', probs.astype(jnp.float32), keys[:, :, :LAT].astype(jnp.float32)).astype(jnp.bfloat16)
    latent = latent.reshape(TOKENS, HEADS, LAT)
    v_out = jnp.einsum('thc,hcv->thv', latent.astype(jnp.float32), w_uv.astype(jnp.float32)).astype(jnp.bfloat16)
    attn = jnp.dot(v_out.reshape(TOKENS, HEADS * VDIM), w_out, preferred_element_type=jnp.float32)
    stream = residual.astype(jnp.float32) + attn
    normed = (stream * lax.rsqrt(lax.optimization_barrier(jnp.mean(stream * stream, axis=-1, keepdims=True)) + 1e-06) * norm_gain).astype(jnp.bfloat16)
    pairs = TOK_DEV * TOPK
    ids_dev = route_ids.reshape(N_EP, pairs)
    gates_dev = route_gates.reshape(N_EP, pairs)
    onehot = (ids_dev[:, :, None] == jnp.arange(EXPERTS, dtype=jnp.int32)[None, None, :]).astype(jnp.int32)
    ranked = jnp.cumsum(onehot, axis=1) - onehot
    slot_of = lax.optimization_barrier(jnp.sum(ranked * onehot, axis=-1))
    token_of = (jnp.arange(N_EP, dtype=jnp.int32)[:, None] * TOK_DEV + jnp.arange(pairs, dtype=jnp.int32)[None, :] // TOPK).astype(jnp.int32)
    token_map = (jnp.arange(pairs)[:, None] // TOPK == jnp.arange(TOK_DEV)[None, :]).astype(jnp.float32)
    moe = jnp.zeros((N_EP, TOK_DEV, D), jnp.float32)
    for expert in range(EXPERTS):
        chosen = (ids_dev[:, None, :] == expert) & (slot_of[:, None, :] == jnp.arange(CAP)[None, :, None])
        filled = jnp.any(chosen, axis=-1)
        index = lax.optimization_barrier(jnp.sum(jnp.where(chosen, token_of[:, None, :], 0), axis=-1)).astype(jnp.int32)
        picked = jnp.where(filled[:, :, None], normed[index.reshape(-1)].reshape(N_EP, CAP, D), jnp.zeros((), jnp.bfloat16))
        picked = picked.reshape(N_EP * CAP, D)
        columns = slice(expert * EXP_HID, (expert + 1) * EXP_HID)
        gate = jnp.dot(picked, w_gate[:, columns], preferred_element_type=jnp.float32)
        upward = jnp.dot(picked, w_up[:, columns], preferred_element_type=jnp.float32)
        act = (jax.nn.silu(gate) * upward).astype(jnp.bfloat16)
        part = jnp.einsum('rjk,jkd->rjd', act.reshape(N_EP * CAP, SPLIT, HID_DEV).astype(jnp.float32), w_down[columns].reshape(SPLIT, HID_DEV, D).astype(jnp.float32)).astype(jnp.bfloat16)
        summed = lax.optimization_barrier(jnp.sum(part.astype(jnp.float32), axis=1)).reshape(N_EP, CAP, D)
        weights = jnp.where(chosen, gates_dev[:, None, :], 0.0)
        mixing = jnp.einsum('scq,qt->stc', weights, token_map, precision=lax.Precision.HIGHEST)
        moe = moe + jnp.einsum('stc,scd->std', mixing, summed, precision=lax.Precision.HIGHEST)
    return (attn.astype(jnp.bfloat16), moe.reshape(TOKENS, D).astype(jnp.bfloat16))
```

```python
import functools

import jax
import jax.numpy as jnp
from jax import lax
from jax.experimental import pallas as pl
from jax.experimental.pallas import tpu as pltpu
from jax.sharding import PartitionSpec as P

EXPERTS = 8


def latent_attention(q_home, new_kv, kv_cache, lengths, scale, lat_width):
    req_dev, seq_len, width = kv_cache.shape
    groups, rows, _ = q_home.shape
    part = rows // req_dev
    q_req = q_home.reshape(groups, req_dev, part, width)
    fresh = new_kv.reshape(req_dev, 2, width)
    old = jnp.einsum("grqc,rkc->rgqk", q_req, kv_cache, preferred_element_type=jnp.float32)
    new = jnp.einsum("grqc,rkc->rgqk", q_req, fresh, preferred_element_type=jnp.float32)
    draft = jnp.arange(part) // (part // 2)
    keep_old = (jnp.arange(seq_len) < lengths[:, None])[:, None, None, :]
    keep_new = (jnp.arange(2)[None, :] <= draft[:, None])[None, None]
    old = jnp.where(keep_old, old * scale, -1e30)
    new = jnp.where(keep_new, new * scale, -1e30)
    highest = jnp.maximum(
        jnp.max(old, axis=-1, keepdims=True), jnp.max(new, axis=-1, keepdims=True)
    )
    old = jnp.where(keep_old, jnp.exp(old - highest), 0.0)
    new = jnp.where(keep_new, jnp.exp(new - highest), 0.0)
    total = jnp.sum(old, axis=-1, keepdims=True) + jnp.sum(new, axis=-1, keepdims=True)
    old = (old / total).astype(jnp.bfloat16)
    new = (new / total).astype(jnp.bfloat16).astype(jnp.float32)
    latent = jnp.einsum(
        "rgqk,rkc->rgqc", old, kv_cache[:, :, :lat_width], preferred_element_type=jnp.float32
    )
    tail = fresh[:, None, None, :, :lat_width].astype(jnp.float32)
    latent = latent + new[..., 0:1] * tail[..., 0, :] + new[..., 1:2] * tail[..., 1, :]
    latent = latent.astype(jnp.bfloat16)
    return jnp.transpose(latent, (1, 0, 2, 3)).reshape(groups, rows, lat_width)


def exchange_kernel(n, share, in_ref, out_ref, send_sem, recv_sem, own_sem):
    me = lax.axis_index("ep")
    barrier = pltpu.get_barrier_semaphore()

    def greet(k, carry):
        pl.semaphore_signal(
            barrier,
            inc=1,
            device_id={"ep": lax.rem(me + k, n)},
            device_id_type=pl.DeviceIdType.MESH,
        )
        return carry

    lax.fori_loop(1, n, greet, 0)
    own = pltpu.make_async_copy(in_ref.at[me // share], out_ref.at[me], own_sem)
    own.start()
    pl.semaphore_wait(barrier, n - 1)

    def copy(k):
        target = lax.rem(me + k, n)
        return pltpu.make_async_remote_copy(
            src_ref=in_ref.at[target // share],
            dst_ref=out_ref.at[me],
            send_sem=send_sem.at[k],
            recv_sem=recv_sem.at[k],
            device_id={"ep": target},
            device_id_type=pl.DeviceIdType.MESH,
        )

    def start(k, carry):
        copy(k).start()
        return carry

    def finish(k, carry):
        copy(k).wait()
        return carry

    lax.fori_loop(1, n, start, 0)
    own.wait()
    lax.fori_loop(1, n, finish, 0)


def exchange(blocks, number, share=1):
    n = blocks.shape[0] * share
    shape = (n,) + blocks.shape[1:]
    return pl.pallas_call(
        functools.partial(exchange_kernel, n, share),
        out_shape=jax.ShapeDtypeStruct(shape, blocks.dtype),
        in_specs=[pl.BlockSpec(memory_space=pltpu.VMEM)],
        out_specs=pl.BlockSpec(memory_space=pltpu.VMEM),
        scratch_shapes=[
            pltpu.SemaphoreType.DMA((n,)),
            pltpu.SemaphoreType.DMA((n,)),
            pltpu.SemaphoreType.DMA,
        ],
        compiler_params=pltpu.CompilerParams(
            collective_id=number, has_side_effects=True, vmem_limit_bytes=32 * 2**20
        ),
    )(blocks)


def slot_table(flat_ids, experts):
    onehot = (flat_ids[..., None] == jnp.arange(experts, dtype=jnp.int32)).astype(jnp.int32)
    ranked = jnp.cumsum(onehot, axis=-2) - onehot
    return jnp.sum(ranked * onehot, axis=-1)


def shards(
    residual,
    queries,
    new_kv,
    kv_cache,
    lengths,
    w_uk,
    w_uv,
    w_out,
    norm_gain,
    w_gate,
    w_up,
    w_down,
    route_ids,
    route_gates,
):
    dev_count = lax.axis_size("ep")
    nope = w_uk.shape[1]
    lat_width = w_uk.shape[2]
    tok_dev, model = residual.shape
    topk = route_ids.shape[1]
    pairs = tok_dev * topk
    capacity = tok_dev // 2
    split = dev_count // EXPERTS
    scale = queries.shape[2] ** (-0.5)
    q_lat = jnp.einsum(
        "thn,hnc->thc", queries[:, :, :nope], w_uk, preferred_element_type=jnp.float32
    ).astype(jnp.bfloat16)
    q_abs = jnp.concatenate([q_lat, queries[:, :, nope:]], axis=-1)
    heads_dev = q_abs.shape[1]
    q_home = exchange(q_abs.reshape(dev_count, tok_dev * heads_dev, q_abs.shape[2]), 0)
    latent = latent_attention(q_home, new_kv, kv_cache, lengths, scale, lat_width)
    latent_heads = exchange(latent, 1).reshape(dev_count * tok_dev, heads_dev, lat_width)
    v_out = jnp.einsum(
        "thc,hcv->thv", latent_heads, w_uv, preferred_element_type=jnp.float32
    ).astype(jnp.bfloat16)
    v_flat = v_out.reshape(v_out.shape[0], v_out.shape[1] * v_out.shape[2])
    share = jnp.dot(v_flat, w_out, preferred_element_type=jnp.float32).astype(jnp.bfloat16)
    shares = exchange(share.reshape(dev_count, 8 * tok_dev, model // 8), 2)
    attn = jnp.sum(shares.astype(jnp.float32), axis=0).reshape(tok_dev, model)
    stream = residual.astype(jnp.float32) + attn
    normed = (
        stream * lax.rsqrt(jnp.mean(stream * stream, axis=-1, keepdims=True) + 1e-06) * norm_gain
    ).astype(jnp.bfloat16)
    token_map = jnp.arange(pairs)[:, None] // topk == jnp.arange(tok_dev)[None, :]
    own_ids = route_ids.reshape(pairs)
    own_slots = slot_table(own_ids, EXPERTS)
    own_chosen = (own_ids[None, None, :] == jnp.arange(EXPERTS)[:, None, None]) & (
        own_slots[None, None, :] == jnp.arange(capacity)[None, :, None]
    )
    picker = jnp.einsum(
        "ecq,qt->ect",
        own_chosen.astype(jnp.bfloat16),
        token_map.astype(jnp.bfloat16),
        preferred_element_type=jnp.float32,
    ).astype(jnp.bfloat16)
    picked = jnp.dot(
        picker.reshape(EXPERTS * capacity, tok_dev), normed, preferred_element_type=jnp.float32
    ).astype(jnp.bfloat16)
    stacked = exchange(
        picked.reshape(EXPERTS, 8 * capacity, model // 8), 3, share=split
    ).reshape(dev_count * capacity, model)
    gate = jnp.dot(stacked, w_gate, preferred_element_type=jnp.float32)
    upward = jnp.dot(stacked, w_up, preferred_element_type=jnp.float32)
    act = (jax.nn.silu(gate) * upward).astype(jnp.bfloat16)
    partial_value = jnp.dot(act, w_down, preferred_element_type=jnp.float32).astype(jnp.bfloat16)
    returned = exchange(
        partial_value.reshape(dev_count, 8 * capacity, model // 8), 4
    ).reshape(EXPERTS, split, capacity, model)
    summed = jnp.sum(returned.astype(jnp.float32), axis=1)
    weights = jnp.where(own_chosen, route_gates.reshape(1, 1, pairs), 0.0)
    mixing = jnp.einsum(
        "ecq,qt->tec", weights, token_map.astype(jnp.float32), precision=lax.Precision.HIGHEST
    )
    moe = jnp.einsum("tec,ecd->td", mixing, summed, precision=lax.Precision.HIGHEST)
    return (attn.astype(jnp.bfloat16), moe.astype(jnp.bfloat16))


def solution(mesh):
    return jax.shard_map(
        shards,
        mesh=mesh,
        in_specs=(
            P(("groups", "ep"), None),
            P("groups", "ep", None),
            P(("groups", "ep"), None),
            P(("groups", "ep"), None, None),
            P(("groups", "ep")),
            P("ep", None, None),
            P("ep", None, None),
            P("ep", None),
            P(),
            P(None, "ep"),
            P(None, "ep"),
            P("ep", None),
            P(("groups", "ep"), None),
            P(("groups", "ep"), None),
        ),
        out_specs=(P(("groups", "ep"), None), P(("groups", "ep"), None)),
        check_vma=False,
    )
```

```python
import functools

import jax
import jax.numpy as jnp
from jax import lax
from jax.experimental import pallas as pl
from jax.experimental.pallas import tpu as pltpu
from jax.sharding import PartitionSpec as P

EXPERTS = 8


def latent_attention(q_home, new_kv, kv_cache, lengths, scale, lat_width):
    req_dev, seq_len, width = kv_cache.shape
    groups, rows, _ = q_home.shape
    part = rows // req_dev
    q_req = q_home.reshape(groups, req_dev, part, width)
    fresh = new_kv.reshape(req_dev, 2, width)
    old = jnp.einsum("grqc,rkc->rgqk", q_req, kv_cache, preferred_element_type=jnp.float32)
    new = jnp.einsum("grqc,rkc->rgqk", q_req, fresh, preferred_element_type=jnp.float32)
    draft = jnp.arange(part) // (part // 2)
    keep_old = (jnp.arange(seq_len) < lengths[:, None])[:, None, None, :]
    keep_new = (jnp.arange(2)[None, :] <= draft[:, None])[None, None]
    old = jnp.where(keep_old, old * scale, -1e30)
    new = jnp.where(keep_new, new * scale, -1e30)
    highest = jnp.maximum(
        jnp.max(old, axis=-1, keepdims=True), jnp.max(new, axis=-1, keepdims=True)
    )
    old = jnp.where(keep_old, jnp.exp(old - highest), 0.0)
    new = jnp.where(keep_new, jnp.exp(new - highest), 0.0)
    total = jnp.sum(old, axis=-1, keepdims=True) + jnp.sum(new, axis=-1, keepdims=True)
    old = (old / total).astype(jnp.bfloat16)
    new = (new / total).astype(jnp.bfloat16).astype(jnp.float32)
    latent = jnp.einsum(
        "rgqk,rkc->rgqc", old, kv_cache[:, :, :lat_width], preferred_element_type=jnp.float32
    )
    tail = fresh[:, None, None, :, :lat_width].astype(jnp.float32)
    latent = latent + new[..., 0:1] * tail[..., 0, :] + new[..., 1:2] * tail[..., 1, :]
    latent = latent.astype(jnp.bfloat16)
    return jnp.transpose(latent, (1, 0, 2, 3)).reshape(groups, rows, lat_width)


def exchange_kernel(n, in_ref, out_ref, send_sem, recv_sem, own_sem):
    me = lax.axis_index("ep")
    barrier = pltpu.get_barrier_semaphore()

    def greet(k, carry):
        pl.semaphore_signal(
            barrier,
            inc=1,
            device_id={"ep": lax.rem(me + k, n)},
            device_id_type=pl.DeviceIdType.MESH,
        )
        return carry

    lax.fori_loop(1, n, greet, 0)
    own = pltpu.make_async_copy(in_ref.at[me], out_ref.at[me], own_sem)
    own.start()
    pl.semaphore_wait(barrier, n - 1)

    def copy(k):
        target = lax.rem(me + k, n)
        return pltpu.make_async_remote_copy(
            src_ref=in_ref.at[target],
            dst_ref=out_ref.at[me],
            send_sem=send_sem.at[k],
            recv_sem=recv_sem.at[k],
            device_id={"ep": target},
            device_id_type=pl.DeviceIdType.MESH,
        )

    def start(k, carry):
        copy(k).start()
        return carry

    def finish(k, carry):
        copy(k).wait()
        return carry

    lax.fori_loop(1, n, start, 0)
    own.wait()
    lax.fori_loop(1, n, finish, 0)


def exchange(blocks, number):
    n = blocks.shape[0]
    return pl.pallas_call(
        functools.partial(exchange_kernel, n),
        out_shape=jax.ShapeDtypeStruct(blocks.shape, blocks.dtype),
        in_specs=[pl.BlockSpec(memory_space=pltpu.VMEM)],
        out_specs=pl.BlockSpec(memory_space=pltpu.VMEM),
        scratch_shapes=[
            pltpu.SemaphoreType.DMA((n,)),
            pltpu.SemaphoreType.DMA((n,)),
            pltpu.SemaphoreType.DMA,
        ],
        compiler_params=pltpu.CompilerParams(
            collective_id=number, has_side_effects=True, vmem_limit_bytes=32 * 2**20
        ),
    )(blocks)


MESH = pl.DeviceIdType.MESH


def places(half):
    me = lax.axis_index("ep")
    chip, core = me // 2, lax.rem(me, 2)
    return me, chip, core, chip * 2 + 1 - core


def greet_peers(half, chip, core, partner):
    barrier = pltpu.get_barrier_semaphore()

    def greet(k, carry):
        pl.semaphore_signal(
            barrier,
            inc=1,
            device_id={"ep": lax.rem(chip + k, half) * 2 + core},
            device_id_type=MESH,
        )
        return carry

    pl.semaphore_signal(barrier, inc=1, device_id={"ep": partner}, device_id_type=MESH)
    lax.fori_loop(1, half, greet, 0)
    pl.semaphore_wait(barrier, half)


def pair_sum_kernel(
    half, final, in_ref, out_ref, paired, summed, landed, pair_send, pair_recv, send_sem, recv_sem
):
    me, chip, core, partner = places(half)
    greet_peers(half, chip, core, partner)
    place = landed if final else out_ref

    def pair_copy(k):
        at = lax.rem(chip + k, half)
        return pltpu.make_async_remote_copy(
            src_ref=in_ref.at[at * 2 + 1 - core],
            dst_ref=paired.at[at],
            send_sem=pair_send.at[k],
            recv_sem=pair_recv.at[k],
            device_id={"ep": partner},
            device_id_type=MESH,
        )

    def chip_copy(k):
        at = lax.rem(chip + k, half)
        return pltpu.make_async_remote_copy(
            src_ref=summed.at[at],
            dst_ref=place.at[chip],
            send_sem=send_sem.at[k],
            recv_sem=recv_sem.at[k],
            device_id={"ep": at * 2 + core},
            device_id_type=MESH,
        )

    def add(at):
        return in_ref[at * 2 + core].astype(jnp.float32) + paired[at].astype(jnp.float32)

    def begin(k, carry):
        pair_copy(lax.rem(k, half)).start()
        return carry

    def pass_on(k, carry):
        pair_copy(k).wait_recv()
        at = lax.rem(chip + k, half)
        summed[at] = add(at).astype(summed.dtype)
        chip_copy(k).start()
        return carry

    lax.fori_loop(1, half + 1, begin, 0)
    lax.fori_loop(1, half, pass_on, 0)
    pair_copy(0).wait_recv()
    if final:
        out_ref[...] = add(chip)

        def collect(k, carry):
            chip_copy(k).wait_recv()
            out_ref[...] += landed[lax.rem(chip + half - k, half)].astype(jnp.float32)
            return carry

    else:
        out_ref[chip] = add(chip).astype(out_ref.dtype)

        def collect(k, carry):
            chip_copy(k).wait_recv()
            return carry

    def finish(k, carry):
        pair_copy(k).wait_send()
        return carry

    def finish_chip(k, carry):
        chip_copy(k).wait_send()
        return carry

    lax.fori_loop(1, half, collect, 0)
    lax.fori_loop(0, half, finish, 0)
    lax.fori_loop(1, half, finish_chip, 0)


def pair_sum_exchange(blocks, number, final):
    n, rows, columns = blocks.shape
    half = n // 2
    kind = jnp.float32 if final else blocks.dtype
    shape = (rows, columns) if final else (half, rows, columns)
    buffer = pltpu.VMEM((half, rows, columns), blocks.dtype)
    return pl.pallas_call(
        functools.partial(pair_sum_kernel, half, final),
        out_shape=jax.ShapeDtypeStruct(shape, kind),
        in_specs=[pl.BlockSpec(memory_space=pltpu.VMEM)],
        out_specs=pl.BlockSpec(memory_space=pltpu.VMEM),
        scratch_shapes=[buffer, buffer, buffer] + [pltpu.SemaphoreType.DMA((half,))] * 4,
        compiler_params=pltpu.CompilerParams(
            collective_id=number, has_side_effects=True, vmem_limit_bytes=32 * 2**20
        ),
    )(blocks)


def dispatch_kernel(
    half, share, in_ref, out_ref, send_sem, recv_sem, pass_send, pass_recv, own_sem
):
    me, chip, core, partner = places(half)
    own = pltpu.make_async_copy(in_ref.at[chip // share], out_ref.at[me], own_sem)
    own.start()
    greet_peers(half, chip, core, partner)

    def chip_copy(k):
        at = lax.rem(chip + k, half)
        return pltpu.make_async_remote_copy(
            src_ref=in_ref.at[at // share],
            dst_ref=out_ref.at[me],
            send_sem=send_sem.at[k],
            recv_sem=recv_sem.at[k],
            device_id={"ep": at * 2 + core},
            device_id_type=MESH,
        )

    def pass_copy(k):
        source = lax.rem(chip + half - k, half) * 2 + core
        return pltpu.make_async_remote_copy(
            src_ref=out_ref.at[source],
            dst_ref=out_ref.at[source],
            send_sem=pass_send.at[k],
            recv_sem=pass_recv.at[k],
            device_id={"ep": partner},
            device_id_type=MESH,
        )

    def begin(k, carry):
        chip_copy(k).start()
        return carry

    def pass_on(k, carry):
        chip_copy(k).wait_recv()
        pass_copy(k).start()
        return carry

    def finish(k, carry):
        chip_copy(k).wait_send()
        return carry

    def finish_pass(k, carry):
        pass_copy(k).wait()
        return carry

    lax.fori_loop(1, half, begin, 0)
    own.wait()
    pass_copy(0).start()
    lax.fori_loop(1, half, pass_on, 0)
    lax.fori_loop(1, half, finish, 0)
    lax.fori_loop(0, half, finish_pass, 0)


def dispatch(blocks, number, half):
    share = half // blocks.shape[0]
    shape = (2 * half,) + blocks.shape[1:]
    return pl.pallas_call(
        functools.partial(dispatch_kernel, half, share),
        out_shape=jax.ShapeDtypeStruct(shape, blocks.dtype),
        in_specs=[pl.BlockSpec(memory_space=pltpu.VMEM)],
        out_specs=pl.BlockSpec(memory_space=pltpu.VMEM),
        scratch_shapes=[pltpu.SemaphoreType.DMA((half,))] * 4 + [pltpu.SemaphoreType.DMA],
        compiler_params=pltpu.CompilerParams(
            collective_id=number, has_side_effects=True, vmem_limit_bytes=32 * 2**20
        ),
    )(blocks)


def slot_table(flat_ids, experts):
    onehot = (flat_ids[..., None] == jnp.arange(experts, dtype=jnp.int32)).astype(jnp.int32)
    ranked = jnp.cumsum(onehot, axis=-2) - onehot
    return jnp.sum(ranked * onehot, axis=-1)


def shards(
    residual,
    queries,
    new_kv,
    kv_cache,
    lengths,
    w_uk,
    w_uv,
    w_out,
    norm_gain,
    w_gate,
    w_up,
    w_down,
    route_ids,
    route_gates,
):
    dev_count = lax.axis_size("ep")
    nope = w_uk.shape[1]
    lat_width = w_uk.shape[2]
    tok_dev, model = residual.shape
    topk = route_ids.shape[1]
    pairs = tok_dev * topk
    capacity = tok_dev // 2
    split = dev_count // EXPERTS
    scale = queries.shape[2] ** (-0.5)
    q_lat = jnp.einsum(
        "thn,hnc->thc", queries[:, :, :nope], w_uk, preferred_element_type=jnp.float32
    ).astype(jnp.bfloat16)
    q_abs = jnp.concatenate([q_lat, queries[:, :, nope:]], axis=-1)
    heads_dev = q_abs.shape[1]
    q_home = exchange(q_abs.reshape(dev_count, tok_dev * heads_dev, q_abs.shape[2]), 0)
    latent = latent_attention(q_home, new_kv, kv_cache, lengths, scale, lat_width)
    latent_heads = exchange(latent, 1).reshape(dev_count * tok_dev, heads_dev, lat_width)
    v_out = jnp.einsum(
        "thc,hcv->thv", latent_heads, w_uv, preferred_element_type=jnp.float32
    ).astype(jnp.bfloat16)
    v_flat = v_out.reshape(v_out.shape[0], v_out.shape[1] * v_out.shape[2])
    share = jnp.dot(v_flat, w_out, preferred_element_type=jnp.float32).astype(jnp.bfloat16)
    blocks = share.reshape(dev_count, 8 * tok_dev, model // 8)
    attn = pair_sum_exchange(blocks, 2, True).reshape(tok_dev, model)
    stream = residual.astype(jnp.float32) + attn
    normed = (
        stream * lax.rsqrt(jnp.mean(stream * stream, axis=-1, keepdims=True) + 1e-06) * norm_gain
    ).astype(jnp.bfloat16)
    token_map = jnp.arange(pairs)[:, None] // topk == jnp.arange(tok_dev)[None, :]
    own_ids = route_ids.reshape(pairs)
    own_slots = slot_table(own_ids, EXPERTS)
    own_chosen = (own_ids[None, None, :] == jnp.arange(EXPERTS)[:, None, None]) & (
        own_slots[None, None, :] == jnp.arange(capacity)[None, :, None]
    )
    picker = jnp.einsum(
        "ecq,qt->ect",
        own_chosen.astype(jnp.bfloat16),
        token_map.astype(jnp.bfloat16),
        preferred_element_type=jnp.float32,
    ).astype(jnp.bfloat16)
    picked = jnp.dot(
        picker.reshape(EXPERTS * capacity, tok_dev), normed, preferred_element_type=jnp.float32
    ).astype(jnp.bfloat16)
    stacked = dispatch(
        picked.reshape(EXPERTS, 8 * capacity, model // 8), 3, dev_count // 2
    ).reshape(dev_count * capacity, model)
    gate = jnp.dot(stacked, w_gate, preferred_element_type=jnp.float32)
    upward = jnp.dot(stacked, w_up, preferred_element_type=jnp.float32)
    act = (jax.nn.silu(gate) * upward).astype(jnp.bfloat16)
    partial_value = jnp.dot(act, w_down, preferred_element_type=jnp.float32).astype(jnp.bfloat16)
    returned = pair_sum_exchange(
        partial_value.reshape(dev_count, 8 * capacity, model // 8), 4, False
    ).reshape(EXPERTS, split // 2, capacity, model)
    summed = jnp.sum(returned.astype(jnp.float32), axis=1)
    weights = jnp.where(own_chosen, route_gates.reshape(1, 1, pairs), 0.0)
    mixing = jnp.einsum(
        "ecq,qt->tec", weights, token_map.astype(jnp.float32), precision=lax.Precision.HIGHEST
    )
    moe = jnp.einsum("tec,ecd->td", mixing, summed, precision=lax.Precision.HIGHEST)
    return (attn.astype(jnp.bfloat16), moe.astype(jnp.bfloat16))


def solution(mesh):
    return jax.shard_map(
        shards,
        mesh=mesh,
        in_specs=(
            P(("groups", "ep"), None),
            P("groups", "ep", None),
            P(("groups", "ep"), None),
            P(("groups", "ep"), None, None),
            P(("groups", "ep")),
            P("ep", None, None),
            P("ep", None, None),
            P("ep", None),
            P(),
            P(None, "ep"),
            P(None, "ep"),
            P("ep", None),
            P(("groups", "ep"), None),
            P(("groups", "ep"), None),
        ),
        out_specs=(P(("groups", "ep"), None), P(("groups", "ep"), None)),
        check_vma=False,
    )
```

```python
import functools

import jax
import jax.numpy as jnp
from jax import lax
from jax.experimental import pallas as pl
from jax.experimental.pallas import tpu as pltpu
from jax.sharding import PartitionSpec as P

EXPERTS = 8


def latent_attention(q_home, new_kv, kv_cache, lengths, scale, lat_width):
    req_dev, seq_len, width = kv_cache.shape
    groups, rows, _ = q_home.shape
    part = rows // req_dev
    q_req = q_home.reshape(groups, req_dev, part, width)
    fresh = new_kv.reshape(req_dev, 2, width)
    old = jnp.einsum("grqc,rkc->rgqk", q_req, kv_cache, preferred_element_type=jnp.float32)
    new = jnp.einsum("grqc,rkc->rgqk", q_req, fresh, preferred_element_type=jnp.float32)
    draft = jnp.arange(part) // (part // 2)
    keep_old = (jnp.arange(seq_len) < lengths[:, None])[:, None, None, :]
    keep_new = (jnp.arange(2)[None, :] <= draft[:, None])[None, None]
    old = jnp.where(keep_old, old * scale, -1e30)
    new = jnp.where(keep_new, new * scale, -1e30)
    highest = jnp.maximum(
        jnp.max(old, axis=-1, keepdims=True), jnp.max(new, axis=-1, keepdims=True)
    )
    old = jnp.where(keep_old, jnp.exp(old - highest), 0.0)
    new = jnp.where(keep_new, jnp.exp(new - highest), 0.0)
    total = jnp.sum(old, axis=-1, keepdims=True) + jnp.sum(new, axis=-1, keepdims=True)
    old = (old / total).astype(jnp.bfloat16)
    new = (new / total).astype(jnp.bfloat16).astype(jnp.float32)
    latent = jnp.einsum(
        "rgqk,rkc->rgqc", old, kv_cache[:, :, :lat_width], preferred_element_type=jnp.float32
    )
    tail = fresh[:, None, None, :, :lat_width].astype(jnp.float32)
    latent = latent + new[..., 0:1] * tail[..., 0, :] + new[..., 1:2] * tail[..., 1, :]
    latent = latent.astype(jnp.bfloat16)
    return jnp.transpose(latent, (1, 0, 2, 3)).reshape(groups, rows, lat_width)


def exchange_kernel(n, in_ref, out_ref, send_sem, recv_sem, own_sem):
    me = lax.axis_index("ep")
    barrier = pltpu.get_barrier_semaphore()

    def greet(k, carry):
        pl.semaphore_signal(
            barrier,
            inc=1,
            device_id={"ep": lax.rem(me + k, n)},
            device_id_type=pl.DeviceIdType.MESH,
        )
        return carry

    lax.fori_loop(1, n, greet, 0)
    own = pltpu.make_async_copy(in_ref.at[me], out_ref.at[me], own_sem)
    own.start()
    pl.semaphore_wait(barrier, n - 1)

    def copy(k):
        target = lax.rem(me + k, n)
        return pltpu.make_async_remote_copy(
            src_ref=in_ref.at[target],
            dst_ref=out_ref.at[me],
            send_sem=send_sem.at[k],
            recv_sem=recv_sem.at[k],
            device_id={"ep": target},
            device_id_type=pl.DeviceIdType.MESH,
        )

    def start(k, carry):
        copy(k).start()
        return carry

    def finish(k, carry):
        copy(k).wait()
        return carry

    lax.fori_loop(1, n, start, 0)
    own.wait()
    lax.fori_loop(1, n, finish, 0)


def exchange(blocks, number):
    n = blocks.shape[0]
    return pl.pallas_call(
        functools.partial(exchange_kernel, n),
        out_shape=jax.ShapeDtypeStruct(blocks.shape, blocks.dtype),
        in_specs=[pl.BlockSpec(memory_space=pltpu.VMEM)],
        out_specs=pl.BlockSpec(memory_space=pltpu.VMEM),
        scratch_shapes=[
            pltpu.SemaphoreType.DMA((n,)),
            pltpu.SemaphoreType.DMA((n,)),
            pltpu.SemaphoreType.DMA,
        ],
        compiler_params=pltpu.CompilerParams(
            collective_id=number, has_side_effects=True, vmem_limit_bytes=32 * 2**20
        ),
    )(blocks)


MESH = pl.DeviceIdType.MESH
TOGETHER = 4
FRESH_ROWS = 16


def attend_kernel(
    n,
    scale,
    q_ref,
    cache_ref,
    fresh_ref,
    keep_ref,
    out_ref,
    landed,
    latents,
    send_sem,
    recv_sem,
    back_send,
    back_recv,
):
    me = lax.axis_index("ep")
    requests, lat_width = cache_ref.shape[0], out_ref.shape[2]
    part = q_ref.shape[1] // requests
    barrier = pltpu.get_barrier_semaphore()

    def greet(k, carry):
        pl.semaphore_signal(
            barrier, inc=1, device_id={"ep": lax.rem(me + k, n)}, device_id_type=MESH
        )
        return carry

    def copy(k):
        target = lax.rem(me + k, n)
        return pltpu.make_async_remote_copy(
            src_ref=q_ref.at[target],
            dst_ref=landed.at[me],
            send_sem=send_sem.at[k],
            recv_sem=recv_sem.at[k],
            device_id={"ep": target},
            device_id_type=MESH,
        )

    def back(k):
        source = lax.rem(me + n - k, n)
        return pltpu.make_async_remote_copy(
            src_ref=latents.at[source],
            dst_ref=out_ref.at[me],
            send_sem=back_send.at[k],
            recv_sem=back_recv.at[k],
            device_id={"ep": source},
            device_id_type=MESH,
        )

    def attend(sources):
        count = len(sources) * part
        shape = (count, FRESH_ROWS)
        draft = lax.rem(lax.broadcasted_iota(jnp.int32, shape, 0), part) // (part // 2)
        keep_new = lax.broadcasted_iota(jnp.int32, shape, 1) <= draft
        for r in range(requests):
            rows = pl.ds(r * part, part)
            q = jnp.concatenate([landed[s, rows, :] for s in sources], axis=0)
            keys, fresh = cache_ref[r], fresh_ref[r]
            contract = (((1,), (1,)), ((), ()))
            old = lax.dot_general(q, keys, contract, preferred_element_type=jnp.float32)
            new = lax.dot_general(q, fresh, contract, preferred_element_type=jnp.float32)
            keep_old = jnp.broadcast_to(keep_ref[r], old.shape) > 0.5
            old = jnp.where(keep_old, old * scale, -1e30)
            new = jnp.where(keep_new, new * scale, -1e30)
            highest = jnp.maximum(
                jnp.max(old, axis=1, keepdims=True), jnp.max(new, axis=1, keepdims=True)
            )
            old = jnp.where(keep_old, jnp.exp(old - highest), 0.0)
            new = jnp.where(keep_new, jnp.exp(new - highest), 0.0)
            total = jnp.sum(old, axis=1, keepdims=True) + jnp.sum(new, axis=1, keepdims=True)
            old = (old / total).astype(jnp.bfloat16)
            new = (new / total).astype(jnp.bfloat16)
            latent = jnp.dot(old, keys[:, :lat_width], preferred_element_type=jnp.float32)
            latent += jnp.dot(new, fresh[:, :lat_width], preferred_element_type=jnp.float32)
            latent = latent.astype(jnp.bfloat16)
            for i, s in enumerate(sources):
                latents[s, rows, :] = latent[i * part : (i + 1) * part]

    def start(k, carry):
        copy(k).start()
        return carry

    lax.fori_loop(1, n, greet, 0)
    landed[me] = q_ref[me]
    pl.semaphore_wait(barrier, n - 1)
    lax.fori_loop(1, n, start, 0)

    def turn(first, skip):
        for k in range(skip, TOGETHER):
            copy(first + k).wait_recv()
        attend([lax.rem(me + n - first - k, n) for k in range(TOGETHER)])
        for k in range(skip, TOGETHER):
            back(first + k).start()

    def step(group, carry):
        turn(group * TOGETHER, 0)
        return carry

    turn(0, 1)
    out_ref[me] = latents[me]
    lax.fori_loop(1, n // TOGETHER, step, 0)

    def finish(k, carry):
        copy(k).wait_send()
        back(k).wait()
        return carry

    lax.fori_loop(1, n, finish, 0)


def attend_exchange(blocks, new_kv, kv_cache, lengths, scale, lat_width, number):
    n, rows, width = blocks.shape
    requests, seq_len, _ = kv_cache.shape
    fresh = jnp.pad(new_kv.reshape(requests, 2, width), ((0, 0), (0, FRESH_ROWS - 2), (0, 0)))
    keep = (jnp.arange(seq_len) < lengths[:, None]).astype(jnp.float32)[:, None, :]
    return pl.pallas_call(
        functools.partial(attend_kernel, n, scale),
        out_shape=jax.ShapeDtypeStruct((n, rows, lat_width), blocks.dtype),
        in_specs=[pl.BlockSpec(memory_space=pltpu.VMEM)] * 4,
        out_specs=pl.BlockSpec(memory_space=pltpu.VMEM),
        scratch_shapes=[
            pltpu.VMEM((n, rows, width), blocks.dtype),
            pltpu.VMEM((n, rows, lat_width), blocks.dtype),
        ]
        + [pltpu.SemaphoreType.DMA((n,))] * 4,
        compiler_params=pltpu.CompilerParams(
            collective_id=number, has_side_effects=True, vmem_limit_bytes=32 * 2**20
        ),
    )(blocks, kv_cache, fresh, keep)


def places(half):
    me = lax.axis_index("ep")
    chip, core = me // 2, lax.rem(me, 2)
    return me, chip, core, chip * 2 + 1 - core


def greet_peers(half, chip, core, partner):
    barrier = pltpu.get_barrier_semaphore()

    def greet(k, carry):
        pl.semaphore_signal(
            barrier,
            inc=1,
            device_id={"ep": lax.rem(chip + k, half) * 2 + core},
            device_id_type=MESH,
        )
        return carry

    pl.semaphore_signal(barrier, inc=1, device_id={"ep": partner}, device_id_type=MESH)
    lax.fori_loop(1, half, greet, 0)
    pl.semaphore_wait(barrier, half)


def pair_sum_kernel(
    half, final, in_ref, out_ref, paired, summed, landed, pair_send, pair_recv, send_sem, recv_sem
):
    me, chip, core, partner = places(half)
    greet_peers(half, chip, core, partner)
    place = landed if final else out_ref

    def pair_copy(k):
        at = lax.rem(chip + k, half)
        return pltpu.make_async_remote_copy(
            src_ref=in_ref.at[at * 2 + 1 - core],
            dst_ref=paired.at[at],
            send_sem=pair_send.at[k],
            recv_sem=pair_recv.at[k],
            device_id={"ep": partner},
            device_id_type=MESH,
        )

    def chip_copy(k):
        at = lax.rem(chip + k, half)
        return pltpu.make_async_remote_copy(
            src_ref=summed.at[at],
            dst_ref=place.at[chip],
            send_sem=send_sem.at[k],
            recv_sem=recv_sem.at[k],
            device_id={"ep": at * 2 + core},
            device_id_type=MESH,
        )

    def add(at):
        return in_ref[at * 2 + core].astype(jnp.float32) + paired[at].astype(jnp.float32)

    def begin(k, carry):
        pair_copy(lax.rem(k, half)).start()
        return carry

    def pass_on(k, carry):
        pair_copy(k).wait_recv()
        at = lax.rem(chip + k, half)
        summed[at] = add(at).astype(summed.dtype)
        chip_copy(k).start()
        return carry

    lax.fori_loop(1, half + 1, begin, 0)
    lax.fori_loop(1, half, pass_on, 0)
    pair_copy(0).wait_recv()
    if final:
        out_ref[...] = add(chip)

        def collect(k, carry):
            chip_copy(k).wait_recv()
            out_ref[...] += landed[lax.rem(chip + half - k, half)].astype(jnp.float32)
            return carry

    else:
        out_ref[chip] = add(chip).astype(out_ref.dtype)

        def collect(k, carry):
            chip_copy(k).wait_recv()
            return carry

    def finish(k, carry):
        pair_copy(k).wait_send()
        return carry

    def finish_chip(k, carry):
        chip_copy(k).wait_send()
        return carry

    lax.fori_loop(1, half, collect, 0)
    lax.fori_loop(0, half, finish, 0)
    lax.fori_loop(1, half, finish_chip, 0)


def pair_sum_exchange(blocks, number, final):
    n, rows, columns = blocks.shape
    half = n // 2
    kind = jnp.float32 if final else blocks.dtype
    shape = (rows, columns) if final else (half, rows, columns)
    buffer = pltpu.VMEM((half, rows, columns), blocks.dtype)
    return pl.pallas_call(
        functools.partial(pair_sum_kernel, half, final),
        out_shape=jax.ShapeDtypeStruct(shape, kind),
        in_specs=[pl.BlockSpec(memory_space=pltpu.VMEM)],
        out_specs=pl.BlockSpec(memory_space=pltpu.VMEM),
        scratch_shapes=[buffer, buffer, buffer] + [pltpu.SemaphoreType.DMA((half,))] * 4,
        compiler_params=pltpu.CompilerParams(
            collective_id=number, has_side_effects=True, vmem_limit_bytes=32 * 2**20
        ),
    )(blocks)


def dispatch_kernel(
    half, share, in_ref, out_ref, send_sem, recv_sem, pass_send, pass_recv, own_sem
):
    me, chip, core, partner = places(half)
    own = pltpu.make_async_copy(in_ref.at[chip // share], out_ref.at[me], own_sem)
    own.start()
    greet_peers(half, chip, core, partner)

    def chip_copy(k):
        at = lax.rem(chip + k, half)
        return pltpu.make_async_remote_copy(
            src_ref=in_ref.at[at // share],
            dst_ref=out_ref.at[me],
            send_sem=send_sem.at[k],
            recv_sem=recv_sem.at[k],
            device_id={"ep": at * 2 + core},
            device_id_type=MESH,
        )

    def pass_copy(k):
        source = lax.rem(chip + half - k, half) * 2 + core
        return pltpu.make_async_remote_copy(
            src_ref=out_ref.at[source],
            dst_ref=out_ref.at[source],
            send_sem=pass_send.at[k],
            recv_sem=pass_recv.at[k],
            device_id={"ep": partner},
            device_id_type=MESH,
        )

    def begin(k, carry):
        chip_copy(k).start()
        return carry

    def pass_on(k, carry):
        chip_copy(k).wait_recv()
        pass_copy(k).start()
        return carry

    def finish(k, carry):
        chip_copy(k).wait_send()
        return carry

    def finish_pass(k, carry):
        pass_copy(k).wait()
        return carry

    lax.fori_loop(1, half, begin, 0)
    own.wait()
    pass_copy(0).start()
    lax.fori_loop(1, half, pass_on, 0)
    lax.fori_loop(1, half, finish, 0)
    lax.fori_loop(0, half, finish_pass, 0)


def dispatch(blocks, number, half):
    share = half // blocks.shape[0]
    shape = (2 * half,) + blocks.shape[1:]
    return pl.pallas_call(
        functools.partial(dispatch_kernel, half, share),
        out_shape=jax.ShapeDtypeStruct(shape, blocks.dtype),
        in_specs=[pl.BlockSpec(memory_space=pltpu.VMEM)],
        out_specs=pl.BlockSpec(memory_space=pltpu.VMEM),
        scratch_shapes=[pltpu.SemaphoreType.DMA((half,))] * 4 + [pltpu.SemaphoreType.DMA],
        compiler_params=pltpu.CompilerParams(
            collective_id=number, has_side_effects=True, vmem_limit_bytes=32 * 2**20
        ),
    )(blocks)


def slot_table(flat_ids, experts):
    onehot = (flat_ids[..., None] == jnp.arange(experts, dtype=jnp.int32)).astype(jnp.int32)
    ranked = jnp.cumsum(onehot, axis=-2) - onehot
    return jnp.sum(ranked * onehot, axis=-1)


def shards(
    residual,
    queries,
    new_kv,
    kv_cache,
    lengths,
    w_uk,
    w_uv,
    w_out,
    norm_gain,
    w_gate,
    w_up,
    w_down,
    route_ids,
    route_gates,
):
    dev_count = lax.axis_size("ep")
    nope = w_uk.shape[1]
    lat_width = w_uk.shape[2]
    tok_dev, model = residual.shape
    topk = route_ids.shape[1]
    pairs = tok_dev * topk
    capacity = tok_dev // 2
    split = dev_count // EXPERTS
    scale = queries.shape[2] ** (-0.5)
    q_lat = jnp.einsum(
        "thn,hnc->thc", queries[:, :, :nope], w_uk, preferred_element_type=jnp.float32
    ).astype(jnp.bfloat16)
    q_abs = jnp.concatenate([q_lat, queries[:, :, nope:]], axis=-1)
    heads_dev = q_abs.shape[1]
    q_blocks = q_abs.reshape(dev_count, tok_dev * heads_dev, q_abs.shape[2])
    if (2 * heads_dev) % 16 == 0 and dev_count % TOGETHER == 0:
        latents = attend_exchange(q_blocks, new_kv, kv_cache, lengths, scale, lat_width, 5)
    else:
        q_home = exchange(q_blocks, 0)
        latents = exchange(
            latent_attention(q_home, new_kv, kv_cache, lengths, scale, lat_width), 1
        )
    latent_heads = latents.reshape(dev_count * tok_dev, heads_dev, lat_width)
    v_out = jnp.einsum(
        "thc,hcv->thv", latent_heads, w_uv, preferred_element_type=jnp.float32
    ).astype(jnp.bfloat16)
    v_flat = v_out.reshape(v_out.shape[0], v_out.shape[1] * v_out.shape[2])
    share = jnp.dot(v_flat, w_out, preferred_element_type=jnp.float32).astype(jnp.bfloat16)
    blocks = share.reshape(dev_count, 8 * tok_dev, model // 8)
    attn = pair_sum_exchange(blocks, 2, True).reshape(tok_dev, model)
    stream = residual.astype(jnp.float32) + attn
    normed = (
        stream * lax.rsqrt(jnp.mean(stream * stream, axis=-1, keepdims=True) + 1e-06) * norm_gain
    ).astype(jnp.bfloat16)
    token_map = jnp.arange(pairs)[:, None] // topk == jnp.arange(tok_dev)[None, :]
    own_ids = route_ids.reshape(pairs)
    own_slots = slot_table(own_ids, EXPERTS)
    own_chosen = (own_ids[None, None, :] == jnp.arange(EXPERTS)[:, None, None]) & (
        own_slots[None, None, :] == jnp.arange(capacity)[None, :, None]
    )
    picker = jnp.einsum(
        "ecq,qt->ect",
        own_chosen.astype(jnp.bfloat16),
        token_map.astype(jnp.bfloat16),
        preferred_element_type=jnp.float32,
    ).astype(jnp.bfloat16)
    picked = jnp.dot(
        picker.reshape(EXPERTS * capacity, tok_dev), normed, preferred_element_type=jnp.float32
    ).astype(jnp.bfloat16)
    stacked = dispatch(
        picked.reshape(EXPERTS, 8 * capacity, model // 8), 3, dev_count // 2
    ).reshape(dev_count * capacity, model)
    gate = jnp.dot(stacked, w_gate, preferred_element_type=jnp.float32)
    upward = jnp.dot(stacked, w_up, preferred_element_type=jnp.float32)
    act = (jax.nn.silu(gate) * upward).astype(jnp.bfloat16)
    partial_value = jnp.dot(act, w_down, preferred_element_type=jnp.float32).astype(jnp.bfloat16)
    returned = pair_sum_exchange(
        partial_value.reshape(dev_count, 8 * capacity, model // 8), 4, False
    ).reshape(EXPERTS, split // 2, capacity, model)
    summed = jnp.sum(returned.astype(jnp.float32), axis=1)
    weights = jnp.where(own_chosen, route_gates.reshape(1, 1, pairs), 0.0)
    mixing = jnp.einsum(
        "ecq,qt->tec", weights, token_map.astype(jnp.float32), precision=lax.Precision.HIGHEST
    )
    moe = jnp.einsum("tec,ecd->td", mixing, summed, precision=lax.Precision.HIGHEST)
    return (attn.astype(jnp.bfloat16), moe.astype(jnp.bfloat16))


def solution(mesh):
    return jax.shard_map(
        shards,
        mesh=mesh,
        in_specs=(
            P(("groups", "ep"), None),
            P("groups", "ep", None),
            P(("groups", "ep"), None),
            P(("groups", "ep"), None, None),
            P(("groups", "ep")),
            P("ep", None, None),
            P("ep", None, None),
            P("ep", None),
            P(),
            P(None, "ep"),
            P(None, "ep"),
            P("ep", None),
            P(("groups", "ep"), None),
            P(("groups", "ep"), None),
        ),
        out_specs=(P(("groups", "ep"), None), P(("groups", "ep"), None)),
        check_vma=False,
    )
```

```python
import functools

import jax
import jax.numpy as jnp
from jax import lax
from jax.experimental import pallas as pl
from jax.experimental.pallas import tpu as pltpu
from jax.sharding import PartitionSpec as P

EXPERTS = 8


def latent_attention(q_home, new_kv, kv_cache, lengths, scale, lat_width):
    req_dev, seq_len, width = kv_cache.shape
    groups, rows, _ = q_home.shape
    part = rows // req_dev
    q_req = q_home.reshape(groups, req_dev, part, width)
    fresh = new_kv.reshape(req_dev, 2, width)
    old = jnp.einsum("grqc,rkc->rgqk", q_req, kv_cache, preferred_element_type=jnp.float32)
    new = jnp.einsum("grqc,rkc->rgqk", q_req, fresh, preferred_element_type=jnp.float32)
    draft = jnp.arange(part) // (part // 2)
    keep_old = (jnp.arange(seq_len) < lengths[:, None])[:, None, None, :]
    keep_new = (jnp.arange(2)[None, :] <= draft[:, None])[None, None]
    old = jnp.where(keep_old, old * scale, -1e30)
    new = jnp.where(keep_new, new * scale, -1e30)
    highest = jnp.maximum(
        jnp.max(old, axis=-1, keepdims=True), jnp.max(new, axis=-1, keepdims=True)
    )
    old = jnp.where(keep_old, jnp.exp(old - highest), 0.0)
    new = jnp.where(keep_new, jnp.exp(new - highest), 0.0)
    total = jnp.sum(old, axis=-1, keepdims=True) + jnp.sum(new, axis=-1, keepdims=True)
    old = (old / total).astype(jnp.bfloat16)
    new = (new / total).astype(jnp.bfloat16).astype(jnp.float32)
    latent = jnp.einsum(
        "rgqk,rkc->rgqc", old, kv_cache[:, :, :lat_width], preferred_element_type=jnp.float32
    )
    tail = fresh[:, None, None, :, :lat_width].astype(jnp.float32)
    latent = latent + new[..., 0:1] * tail[..., 0, :] + new[..., 1:2] * tail[..., 1, :]
    latent = latent.astype(jnp.bfloat16)
    return jnp.transpose(latent, (1, 0, 2, 3)).reshape(groups, rows, lat_width)


def exchange_kernel(n, in_ref, out_ref, send_sem, recv_sem, own_sem):
    me = lax.axis_index("ep")
    barrier = pltpu.get_barrier_semaphore()

    def greet(k, carry):
        pl.semaphore_signal(
            barrier,
            inc=1,
            device_id={"ep": lax.rem(me + k, n)},
            device_id_type=pl.DeviceIdType.MESH,
        )
        return carry

    lax.fori_loop(1, n, greet, 0)
    own = pltpu.make_async_copy(in_ref.at[me], out_ref.at[me], own_sem)
    own.start()
    pl.semaphore_wait(barrier, n - 1)

    def copy(k):
        target = lax.rem(me + k, n)
        return pltpu.make_async_remote_copy(
            src_ref=in_ref.at[target],
            dst_ref=out_ref.at[me],
            send_sem=send_sem.at[k],
            recv_sem=recv_sem.at[k],
            device_id={"ep": target},
            device_id_type=pl.DeviceIdType.MESH,
        )

    def start(k, carry):
        copy(k).start()
        return carry

    def finish(k, carry):
        copy(k).wait()
        return carry

    lax.fori_loop(1, n, start, 0)
    own.wait()
    lax.fori_loop(1, n, finish, 0)


def exchange(blocks, number):
    n = blocks.shape[0]
    return pl.pallas_call(
        functools.partial(exchange_kernel, n),
        out_shape=jax.ShapeDtypeStruct(blocks.shape, blocks.dtype),
        in_specs=[pl.BlockSpec(memory_space=pltpu.VMEM)],
        out_specs=pl.BlockSpec(memory_space=pltpu.VMEM),
        scratch_shapes=[
            pltpu.SemaphoreType.DMA((n,)),
            pltpu.SemaphoreType.DMA((n,)),
            pltpu.SemaphoreType.DMA,
        ],
        compiler_params=pltpu.CompilerParams(
            collective_id=number, has_side_effects=True, vmem_limit_bytes=32 * 2**20
        ),
    )(blocks)


MESH = pl.DeviceIdType.MESH
TOGETHER = 4
FRESH_ROWS = 16


def attend_kernel(
    n,
    scale,
    q_ref,
    cache_ref,
    fresh_ref,
    keep_ref,
    out_ref,
    landed,
    latents,
    send_sem,
    recv_sem,
    back_send,
    back_recv,
):
    me = lax.axis_index("ep")
    requests, lat_width = cache_ref.shape[0], out_ref.shape[2]
    part = q_ref.shape[1] // requests
    barrier = pltpu.get_barrier_semaphore()

    def greet(k, carry):
        pl.semaphore_signal(
            barrier, inc=1, device_id={"ep": lax.rem(me + k, n)}, device_id_type=MESH
        )
        return carry

    def copy(k):
        target = lax.rem(me + k, n)
        return pltpu.make_async_remote_copy(
            src_ref=q_ref.at[target],
            dst_ref=landed.at[me],
            send_sem=send_sem.at[k],
            recv_sem=recv_sem.at[k],
            device_id={"ep": target},
            device_id_type=MESH,
        )

    def back(k):
        source = lax.rem(me + n - k, n)
        return pltpu.make_async_remote_copy(
            src_ref=latents.at[source],
            dst_ref=out_ref.at[me],
            send_sem=back_send.at[k],
            recv_sem=back_recv.at[k],
            device_id={"ep": source},
            device_id_type=MESH,
        )

    def attend(sources):
        count = len(sources) * part
        shape = (count, FRESH_ROWS)
        draft = lax.rem(lax.broadcasted_iota(jnp.int32, shape, 0), part) // (part // 2)
        keep_new = lax.broadcasted_iota(jnp.int32, shape, 1) <= draft
        for r in range(requests):
            rows = pl.ds(r * part, part)
            q = jnp.concatenate([landed[s, rows, :] for s in sources], axis=0)
            keys, fresh = cache_ref[r], fresh_ref[r]
            contract = (((1,), (1,)), ((), ()))
            old = lax.dot_general(q, keys, contract, preferred_element_type=jnp.float32)
            new = lax.dot_general(q, fresh, contract, preferred_element_type=jnp.float32)
            keep_old = jnp.broadcast_to(keep_ref[r], old.shape) > 0.5
            old = jnp.where(keep_old, old * scale, -1e30)
            new = jnp.where(keep_new, new * scale, -1e30)
            highest = jnp.maximum(
                jnp.max(old, axis=1, keepdims=True), jnp.max(new, axis=1, keepdims=True)
            )
            old = jnp.where(keep_old, jnp.exp(old - highest), 0.0)
            new = jnp.where(keep_new, jnp.exp(new - highest), 0.0)
            total = jnp.sum(old, axis=1, keepdims=True) + jnp.sum(new, axis=1, keepdims=True)
            old = (old / total).astype(jnp.bfloat16)
            new = (new / total).astype(jnp.bfloat16)
            latent = jnp.dot(old, keys[:, :lat_width], preferred_element_type=jnp.float32)
            latent += jnp.dot(new, fresh[:, :lat_width], preferred_element_type=jnp.float32)
            latent = latent.astype(jnp.bfloat16)
            for i, s in enumerate(sources):
                latents[s, rows, :] = latent[i * part : (i + 1) * part]

    def start(k, carry):
        copy(k).start()
        return carry

    lax.fori_loop(1, n, greet, 0)
    landed[me] = q_ref[me]
    pl.semaphore_wait(barrier, n - 1)
    lax.fori_loop(1, 2 * TOGETHER, start, 0)

    def turn(first, skip):
        for k in range(skip, TOGETHER):
            copy(first + k).wait_recv()
        ahead = first + 2 * TOGETHER
        if ahead < n:
            lax.fori_loop(ahead, ahead + TOGETHER, start, 0)
        attend([lax.rem(me + n - first - k, n) for k in range(TOGETHER)])
        for k in range(skip, TOGETHER):
            back(first + k).start()

    turn(0, 1)
    out_ref[me] = latents[me]
    for group in range(1, n // TOGETHER):
        turn(group * TOGETHER, 0)

    def finish(k, carry):
        copy(k).wait_send()
        back(k).wait()
        return carry

    lax.fori_loop(1, n, finish, 0)


def attend_exchange(blocks, new_kv, kv_cache, lengths, scale, lat_width, number):
    n, rows, width = blocks.shape
    requests, seq_len, _ = kv_cache.shape
    fresh = jnp.pad(new_kv.reshape(requests, 2, width), ((0, 0), (0, FRESH_ROWS - 2), (0, 0)))
    keep = (jnp.arange(seq_len) < lengths[:, None]).astype(jnp.float32)[:, None, :]
    return pl.pallas_call(
        functools.partial(attend_kernel, n, scale),
        out_shape=jax.ShapeDtypeStruct((n, rows, lat_width), blocks.dtype),
        in_specs=[pl.BlockSpec(memory_space=pltpu.VMEM)] * 4,
        out_specs=pl.BlockSpec(memory_space=pltpu.VMEM),
        scratch_shapes=[
            pltpu.VMEM((n, rows, width), blocks.dtype),
            pltpu.VMEM((n, rows, lat_width), blocks.dtype),
        ]
        + [pltpu.SemaphoreType.DMA((n,))] * 4,
        compiler_params=pltpu.CompilerParams(
            collective_id=number, has_side_effects=True, vmem_limit_bytes=32 * 2**20
        ),
    )(blocks, kv_cache, fresh, keep)


def places(half):
    me = lax.axis_index("ep")
    chip, core = me // 2, lax.rem(me, 2)
    return me, chip, core, chip * 2 + 1 - core


def greet_peers(half, chip, core, partner):
    barrier = pltpu.get_barrier_semaphore()

    def greet(k, carry):
        pl.semaphore_signal(
            barrier,
            inc=1,
            device_id={"ep": lax.rem(chip + k, half) * 2 + core},
            device_id_type=MESH,
        )
        return carry

    pl.semaphore_signal(barrier, inc=1, device_id={"ep": partner}, device_id_type=MESH)
    lax.fori_loop(1, half, greet, 0)
    pl.semaphore_wait(barrier, half)


def pair_sum_kernel(
    half, final, in_ref, out_ref, paired, summed, landed, pair_send, pair_recv, send_sem, recv_sem
):
    me, chip, core, partner = places(half)
    greet_peers(half, chip, core, partner)
    place = landed if final else out_ref

    def pair_copy(k):
        at = lax.rem(chip + k, half)
        return pltpu.make_async_remote_copy(
            src_ref=in_ref.at[at * 2 + 1 - core],
            dst_ref=paired.at[at],
            send_sem=pair_send.at[k],
            recv_sem=pair_recv.at[k],
            device_id={"ep": partner},
            device_id_type=MESH,
        )

    def chip_copy(k):
        at = lax.rem(chip + k, half)
        return pltpu.make_async_remote_copy(
            src_ref=summed.at[at],
            dst_ref=place.at[chip],
            send_sem=send_sem.at[k],
            recv_sem=recv_sem.at[k],
            device_id={"ep": at * 2 + core},
            device_id_type=MESH,
        )

    def add(at):
        return in_ref[at * 2 + core].astype(jnp.float32) + paired[at].astype(jnp.float32)

    def begin(k, carry):
        pair_copy(lax.rem(k, half)).start()
        return carry

    def pass_on(k, carry):
        pair_copy(k).wait_recv()
        at = lax.rem(chip + k, half)
        summed[at] = add(at).astype(summed.dtype)
        chip_copy(k).start()
        return carry

    lax.fori_loop(1, half + 1, begin, 0)
    lax.fori_loop(1, half, pass_on, 0)
    pair_copy(0).wait_recv()
    if final:
        out_ref[...] = add(chip)

        def collect(k, carry):
            chip_copy(k).wait_recv()
            out_ref[...] += landed[lax.rem(chip + half - k, half)].astype(jnp.float32)
            return carry

    else:
        out_ref[chip] = add(chip).astype(out_ref.dtype)

        def collect(k, carry):
            chip_copy(k).wait_recv()
            return carry

    def finish(k, carry):
        pair_copy(k).wait_send()
        return carry

    def finish_chip(k, carry):
        chip_copy(k).wait_send()
        return carry

    lax.fori_loop(1, half, collect, 0)
    lax.fori_loop(0, half, finish, 0)
    lax.fori_loop(1, half, finish_chip, 0)


def pair_sum_exchange(blocks, number, final):
    n, rows, columns = blocks.shape
    half = n // 2
    kind = jnp.float32 if final else blocks.dtype
    shape = (rows, columns) if final else (half, rows, columns)
    buffer = pltpu.VMEM((half, rows, columns), blocks.dtype)
    return pl.pallas_call(
        functools.partial(pair_sum_kernel, half, final),
        out_shape=jax.ShapeDtypeStruct(shape, kind),
        in_specs=[pl.BlockSpec(memory_space=pltpu.VMEM)],
        out_specs=pl.BlockSpec(memory_space=pltpu.VMEM),
        scratch_shapes=[buffer, buffer, buffer] + [pltpu.SemaphoreType.DMA((half,))] * 4,
        compiler_params=pltpu.CompilerParams(
            collective_id=number, has_side_effects=True, vmem_limit_bytes=32 * 2**20
        ),
    )(blocks)


def dispatch_kernel(
    half, share, in_ref, out_ref, send_sem, recv_sem, pass_send, pass_recv, own_sem
):
    me, chip, core, partner = places(half)
    own = pltpu.make_async_copy(in_ref.at[chip // share], out_ref.at[me], own_sem)
    own.start()
    greet_peers(half, chip, core, partner)

    def chip_copy(k):
        at = lax.rem(chip + k, half)
        return pltpu.make_async_remote_copy(
            src_ref=in_ref.at[at // share],
            dst_ref=out_ref.at[me],
            send_sem=send_sem.at[k],
            recv_sem=recv_sem.at[k],
            device_id={"ep": at * 2 + core},
            device_id_type=MESH,
        )

    def pass_copy(k):
        source = lax.rem(chip + half - k, half) * 2 + core
        return pltpu.make_async_remote_copy(
            src_ref=out_ref.at[source],
            dst_ref=out_ref.at[source],
            send_sem=pass_send.at[k],
            recv_sem=pass_recv.at[k],
            device_id={"ep": partner},
            device_id_type=MESH,
        )

    def begin(k, carry):
        chip_copy(k).start()
        return carry

    def pass_on(k, carry):
        chip_copy(k).wait_recv()
        pass_copy(k).start()
        return carry

    def finish(k, carry):
        chip_copy(k).wait_send()
        return carry

    def finish_pass(k, carry):
        pass_copy(k).wait()
        return carry

    lax.fori_loop(1, half, begin, 0)
    own.wait()
    pass_copy(0).start()
    lax.fori_loop(1, half, pass_on, 0)
    lax.fori_loop(1, half, finish, 0)
    lax.fori_loop(0, half, finish_pass, 0)


def dispatch(blocks, number, half):
    share = half // blocks.shape[0]
    shape = (2 * half,) + blocks.shape[1:]
    return pl.pallas_call(
        functools.partial(dispatch_kernel, half, share),
        out_shape=jax.ShapeDtypeStruct(shape, blocks.dtype),
        in_specs=[pl.BlockSpec(memory_space=pltpu.VMEM)],
        out_specs=pl.BlockSpec(memory_space=pltpu.VMEM),
        scratch_shapes=[pltpu.SemaphoreType.DMA((half,))] * 4 + [pltpu.SemaphoreType.DMA],
        compiler_params=pltpu.CompilerParams(
            collective_id=number, has_side_effects=True, vmem_limit_bytes=32 * 2**20
        ),
    )(blocks)


def slot_table(flat_ids, experts):
    onehot = (flat_ids[..., None] == jnp.arange(experts, dtype=jnp.int32)).astype(jnp.int32)
    ranked = jnp.cumsum(onehot, axis=-2) - onehot
    return jnp.sum(ranked * onehot, axis=-1)


def shards(
    residual,
    queries,
    new_kv,
    kv_cache,
    lengths,
    w_uk,
    w_uv,
    w_out,
    norm_gain,
    w_gate,
    w_up,
    w_down,
    route_ids,
    route_gates,
):
    dev_count = lax.axis_size("ep")
    nope = w_uk.shape[1]
    lat_width = w_uk.shape[2]
    tok_dev, model = residual.shape
    topk = route_ids.shape[1]
    pairs = tok_dev * topk
    capacity = tok_dev // 2
    split = dev_count // EXPERTS
    scale = queries.shape[2] ** (-0.5)
    q_lat = jnp.einsum(
        "thn,hnc->thc", queries[:, :, :nope], w_uk, preferred_element_type=jnp.float32
    ).astype(jnp.bfloat16)
    q_abs = jnp.concatenate([q_lat, queries[:, :, nope:]], axis=-1)
    heads_dev = q_abs.shape[1]
    q_blocks = q_abs.reshape(dev_count, tok_dev * heads_dev, q_abs.shape[2])
    if (2 * heads_dev) % 16 == 0 and dev_count % TOGETHER == 0 and dev_count >= 2 * TOGETHER:
        latents = attend_exchange(q_blocks, new_kv, kv_cache, lengths, scale, lat_width, 5)
    else:
        q_home = exchange(q_blocks, 0)
        latents = exchange(
            latent_attention(q_home, new_kv, kv_cache, lengths, scale, lat_width), 1
        )
    latent_heads = latents.reshape(dev_count * tok_dev, heads_dev, lat_width)
    v_out = jnp.einsum(
        "thc,hcv->thv", latent_heads, w_uv, preferred_element_type=jnp.float32
    ).astype(jnp.bfloat16)
    v_flat = v_out.reshape(v_out.shape[0], v_out.shape[1] * v_out.shape[2])
    share = jnp.dot(v_flat, w_out, preferred_element_type=jnp.float32).astype(jnp.bfloat16)
    blocks = share.reshape(dev_count, 8 * tok_dev, model // 8)
    attn = pair_sum_exchange(blocks, 2, True).reshape(tok_dev, model)
    stream = residual.astype(jnp.float32) + attn
    normed = (
        stream * lax.rsqrt(jnp.mean(stream * stream, axis=-1, keepdims=True) + 1e-06) * norm_gain
    ).astype(jnp.bfloat16)
    token_map = jnp.arange(pairs)[:, None] // topk == jnp.arange(tok_dev)[None, :]
    own_ids = route_ids.reshape(pairs)
    own_slots = slot_table(own_ids, EXPERTS)
    own_chosen = (own_ids[None, None, :] == jnp.arange(EXPERTS)[:, None, None]) & (
        own_slots[None, None, :] == jnp.arange(capacity)[None, :, None]
    )
    picker = jnp.einsum(
        "ecq,qt->ect",
        own_chosen.astype(jnp.bfloat16),
        token_map.astype(jnp.bfloat16),
        preferred_element_type=jnp.float32,
    ).astype(jnp.bfloat16)
    picked = jnp.dot(
        picker.reshape(EXPERTS * capacity, tok_dev), normed, preferred_element_type=jnp.float32
    ).astype(jnp.bfloat16)
    stacked = dispatch(
        picked.reshape(EXPERTS, 8 * capacity, model // 8), 3, dev_count // 2
    ).reshape(dev_count * capacity, model)
    gate = jnp.dot(stacked, w_gate, preferred_element_type=jnp.float32)
    upward = jnp.dot(stacked, w_up, preferred_element_type=jnp.float32)
    act = (jax.nn.silu(gate) * upward).astype(jnp.bfloat16)
    partial_value = jnp.dot(act, w_down, preferred_element_type=jnp.float32).astype(jnp.bfloat16)
    returned = pair_sum_exchange(
        partial_value.reshape(dev_count, 8 * capacity, model // 8), 4, False
    ).reshape(EXPERTS, split // 2, capacity, model)
    summed = jnp.sum(returned.astype(jnp.float32), axis=1)
    weights = jnp.where(own_chosen, route_gates.reshape(1, 1, pairs), 0.0)
    mixing = jnp.einsum(
        "ecq,qt->tec", weights, token_map.astype(jnp.float32), precision=lax.Precision.HIGHEST
    )
    moe = jnp.einsum("tec,ecd->td", mixing, summed, precision=lax.Precision.HIGHEST)
    return (attn.astype(jnp.bfloat16), moe.astype(jnp.bfloat16))


def solution(mesh):
    return jax.shard_map(
        shards,
        mesh=mesh,
        in_specs=(
            P(("groups", "ep"), None),
            P("groups", "ep", None),
            P(("groups", "ep"), None),
            P(("groups", "ep"), None, None),
            P(("groups", "ep")),
            P("ep", None, None),
            P("ep", None, None),
            P("ep", None),
            P(),
            P(None, "ep"),
            P(None, "ep"),
            P("ep", None),
            P(("groups", "ep"), None),
            P(("groups", "ep"), None),
        ),
        out_specs=(P(("groups", "ep"), None), P(("groups", "ep"), None)),
        check_vma=False,
    )
```
